1024 devices in a mesh: dp: 8 (over x_lo, core), expert: 8 (over z), etensor: 16 (over y, x_hi).
Axes of the slice: x: 8 (x_hi: 2, x_lo: 4; x = x_hi * 4 + x_lo), y: 8, z: 8, core: 2. Of those that a mesh axis runs over, the one named last changes fastest.
Arguments:
- tokens: bfloat16 [4096, 3072], P(('dp', 'expert', 'etensor')), may hold values from -6 to 6
- routes: int32 [4096, 2], P(('dp', 'expert', 'etensor')), may hold values from 0 to 7, as said below
- up_weight: bfloat16 [8, 3072, 16384], P('expert', 'dp', 'etensor'), may hold values from -0.046875 to 0.046875
- hidden_grad: bfloat16 [8, 1024, 16384], P('expert', 'dp', 'etensor'), may hold values from -6 to 6
- gate_pre: bfloat16 [8, 1024, 16384], P('expert', 'dp', 'etensor'), may hold values from -8 to 8
Outputs:
- grad_tokens: bfloat16 [4096, 3072], P(('dp', 'expert', 'etensor'))
- grad_up_weight: bfloat16 [8, 3072, 16384], P('expert', 'dp', 'etensor')
The draws below stay inside these ranges and needn't reach their ends.
Inputs may be any that keep to these rules, and one draw needn't show every extreme that they name: `routes`: among the 8 picks of one device every expert is named exactly 1 times, and a token names 2 different experts.
All inputs are finite; a program needn't handle non-finite values.
Results may differ from the reference program's by a relative error of at most 0.0059.
Values may be sent and summed in bfloat16 or wider, within the bound.
No kernel may reach another device: no remote copies, remote signals or barrier semaphores. Data moves between devices by JAX's collectives and lax.ppermute only.
A program may use at most 32 MiB of HBM per device.

```python
import jax
import jax.numpy as jnp
from jax import lax

D = 3072
FF = 16384
TOP = 2
TOK_DEV = 4
EXPERTS = 8
SLOTS = 1
ROWS = 1024
TOKENS = 4096
DEVICES = 1024


def draw_routes(key, part):
    key = jax.random.fold_in(key, 7)
    perm_keys = jax.random.split(key, DEVICES + 1)
    orders = jax.vmap(lambda sub: jax.random.permutation(sub, EXPERTS))(perm_keys[:DEVICES])
    offsets = jax.random.randint(perm_keys[DEVICES], (DEVICES, 1), 0, EXPERTS)
    positions = (offsets + jnp.arange(TOK_DEV * TOP, dtype=jnp.int32)[None, :]) % EXPERTS
    chosen = jnp.take_along_axis(orders.astype(jnp.int32), positions.astype(jnp.int32), axis=1)
    return chosen.reshape(DEVICES * TOK_DEV, TOP).astype(jnp.int32)


def steps_of(stream_key, extent, shards, low, largest):
    def one(position, blocks):
        steps = jax.random.uniform(jax.random.fold_in(jax.random.fold_in(stream_key, 6), position), (blocks,), jnp.float32, low / len(shards), largest / len(shards))
        return jnp.repeat(jnp.exp(steps), extent[position] // blocks).reshape((-1,) + (1,) * (len(extent) - position - 1))

    loudness = one(*shards[0])
    for cut in shards[1:]:
        loudness = loudness * one(*cut)
    return loudness


def scatter_about(rng, extent, spread, most, pieces=(), kind=jnp.bfloat16):
    gain = steps_of(rng, extent, pieces, -0.22, 0.18) if pieces else 1.0
    drawn = jax.random.normal(rng, extent, jnp.float32) * spread * gain
    return jnp.minimum(jnp.maximum(drawn, -most), most).astype(kind)


def setup_inputs(seed: int = 0) -> dict:
    keys = jax.random.split(jax.random.key(seed), 6)
    return {
        "tokens": scatter_about(keys[0], (TOKENS, D), 1.0, 6.0, ((0, 1024),)),
        "routes": draw_routes(jax.random.fold_in(keys[5], 71), 0),
        "up_weight": scatter_about(keys[2], (EXPERTS, D, FF), FF ** -0.5, 0.046875, ((0, 8), (1, 8), (2, 16))),
        "hidden_grad": scatter_about(keys[3], (EXPERTS, ROWS, FF), 1.0, 6.0, ((0, 8), (1, 8), (2, 16))),
        "gate_pre": scatter_about(keys[4], (EXPERTS, ROWS, FF), 1.5, 8.0, ((0, 8), (1, 8), (2, 16))),
    }


def slot_layout(routes):
    per_device = TOK_DEV * TOP
    chosen = routes.reshape(DEVICES, per_device).astype(jnp.int32)
    expert_ids = jnp.arange(EXPERTS, dtype=jnp.int32)
    onehot = (chosen[:, :, None] == expert_ids[None, None, :]).astype(jnp.int32)
    ordinal = jnp.sum(jnp.cumsum(onehot, axis=1) * onehot, axis=2) - 1
    device_ids = jnp.arange(DEVICES, dtype=jnp.int32)[:, None]
    pick_ids = jnp.arange(per_device, dtype=jnp.int32)[None, :]
    token_ids = (device_ids * TOK_DEV + pick_ids // TOP).astype(jnp.int32)
    row_ids = (device_ids * SLOTS + ordinal).astype(jnp.int32)
    table = jnp.zeros((EXPERTS, ROWS), jnp.int32).at[chosen, row_ids].set(token_ids)
    return table, (chosen * ROWS + row_ids).astype(jnp.int32)


def expert_backward(operands):
    token_rows, weight_up, grad_hidden, gate_value = operands
    gate_wide = gate_value.astype(jnp.float32)
    sigma = jax.nn.sigmoid(gate_wide)
    grad_up = (grad_hidden.astype(jnp.float32) * gate_wide * sigma).astype(jnp.bfloat16)
    grad_wu = jnp.dot(token_rows.T, grad_up, preferred_element_type=jnp.float32).astype(jnp.bfloat16)
    row_grad = jnp.dot(grad_up, weight_up.T, preferred_element_type=jnp.float32)
    return grad_wu, row_grad.astype(jnp.bfloat16)


def reference(tokens, routes, up_weight, hidden_grad, gate_pre):
    table, pick_rows = slot_layout(routes)
    token_rows = tokens[table]
    grad_wu, row_grad = lax.map(expert_backward, (token_rows, up_weight, hidden_grad, gate_pre))
    flat = row_grad.reshape(EXPERTS * ROWS, D)
    picked = flat[pick_rows.reshape(-1)].astype(jnp.float32).reshape(TOKENS, TOP, D)
    grad_tokens = jnp.sum(picked, axis=1).astype(jnp.bfloat16)
    return grad_tokens, grad_wu
```

```python
import jax
import jax.numpy as jnp
from jax import lax
from jax.sharding import Mesh, PartitionSpec as P

CORE_SWAP = ((0, 1), (1, 0))


def derive(grad_rows, gate_rows):
    gate_wide = gate_rows.astype(jnp.float32)
    sigma = jax.nn.sigmoid(gate_wide)
    return (grad_rows.astype(jnp.float32) * gate_wide * sigma).astype(jnp.bfloat16)


def exchange(blocks, axes):
    return lax.all_to_all(blocks, axes, split_axis=0, concat_axis=0, tiled=True)


def on_device(tokens, routes, up_weight, hidden_grad, gate_pre):
    chips, cores, experts = lax.axis_size("xl"), lax.axis_size("core"), lax.axis_size("ex")
    ys, halves = lax.axis_size("y"), lax.axis_size("h")
    owners = chips * cores
    token_count, width = tokens.shape
    _, shard, hidden = up_weight.shape
    rows = hidden_grad.shape[1]
    inner = halves * experts
    first = lax.axis_index("core") == 0

    grad_up = derive(hidden_grad[0], gate_pre[0])
    grad_up = grad_up.reshape(experts, ys, halves, hidden).transpose(1, 2, 0, 3)
    grad_up = grad_up.reshape(rows, hidden)
    chip_rows = exchange(jnp.broadcast_to(grad_up[None], (chips, rows, hidden)), "xl")
    weight = up_weight[0]
    other_weight = lax.ppermute(weight, "core", CORE_SWAP)
    weights = jnp.concatenate(
        [jnp.where(first, weight, other_weight), jnp.where(first, other_weight, weight)], axis=0
    )

    picks = jnp.any(
        routes[:, :, None] == jnp.arange(experts, dtype=jnp.int32)[None, None, :], axis=1
    ).astype(jnp.bfloat16)
    outgoing = jnp.einsum(
        "te,tqc->qec",
        picks,
        tokens.reshape(token_count, owners, shard),
        preferred_element_type=jnp.float32,
    ).astype(jnp.bfloat16)
    outgoing = jnp.broadcast_to(outgoing[:, None], (owners, halves, experts, shard))
    arrived = exchange(
        outgoing.reshape(owners * halves, experts, shard), ("xl", "core", "h")
    )
    arrived = exchange(arrived.transpose(1, 0, 2), "ex")
    arrived = arrived.reshape(experts, owners, halves, shard).transpose(1, 2, 0, 3)
    arrived = arrived.reshape(owners * inner, shard)

    partial = lax.dot_general(
        chip_rows, weights, (((2,), (1,)), ((), ())), preferred_element_type=jnp.float32
    ).astype(jnp.bfloat16)
    partial = partial.reshape(chips, ys, inner, cores * shard).transpose(1, 0, 2, 3)
    summed = jnp.sum(exchange(partial, "y").astype(jnp.float32), axis=0).astype(jnp.bfloat16)
    summed = exchange(summed.reshape(chips * halves, experts, cores * shard), ("xl", "h"))
    summed = summed.reshape(chips, halves, experts, cores * shard).astype(jnp.float32)
    row_grad = jnp.sum(summed, axis=1).astype(jnp.bfloat16)
    returned = exchange(row_grad.transpose(1, 0, 2), "ex")
    grad_tokens = jnp.einsum(
        "te,eqc->tqc", picks, returned, preferred_element_type=jnp.float32
    ).astype(jnp.bfloat16)

    layer_rows = exchange(jnp.broadcast_to(arrived[None], (ys,) + arrived.shape), "y")
    layer_rows = layer_rows.reshape(ys, chips, cores, inner, shard).transpose(1, 2, 0, 3, 4)
    own_rows = jnp.where(first, layer_rows[:, 0], layer_rows[:, 1]).reshape(chips, rows, shard)
    other_rows = jnp.where(first, layer_rows[:, 1], layer_rows[:, 0]).reshape(chips, rows, shard)
    other_chip_rows = lax.ppermute(chip_rows, "core", CORE_SWAP)
    contract = (((0, 1), (0, 1)), ((), ()))
    weight_grad = lax.dot_general(
        own_rows, chip_rows, contract, preferred_element_type=jnp.float32
    ) + lax.dot_general(
        other_rows, other_chip_rows, contract, preferred_element_type=jnp.float32
    )
    return grad_tokens.reshape(token_count, width), weight_grad.astype(jnp.bfloat16)[None]


def solution(mesh):
    shape = (mesh.shape["dp"] // 2, 2, mesh.shape["expert"], mesh.shape["etensor"] // 2, 2)
    fine = Mesh(mesh.devices.reshape(shape), ("xl", "core", "ex", "y", "h"))
    tokens_spec = P(("xl", "core", "ex", "y", "h"), None)
    expert_spec = P("ex", ("xl", "core"), ("y", "h"))
    return jax.shard_map(
        on_device,
        mesh=fine,
        in_specs=(tokens_spec, tokens_spec, expert_spec, expert_spec, expert_spec),
        out_specs=(tokens_spec, expert_spec),
        check_vma=False,
    )
```

```python
import jax
import jax.numpy as jnp
from jax import lax
from jax.experimental import pallas as pl
from jax.experimental.pallas import tpu as pltpu
from jax.sharding import Mesh, PartitionSpec as P

CORE_SWAP = ((0, 1), (1, 0))
VMEM_BYTES = 40 * 1024 * 1024


def derive(grad_rows, gate_rows):
    gate_wide = gate_rows.astype(jnp.float32)
    sigma = jax.nn.sigmoid(gate_wide)
    return (grad_rows.astype(jnp.float32) * gate_wide * sigma).astype(jnp.bfloat16)


def exchange(blocks, axes):
    return lax.all_to_all(blocks, axes, split_axis=0, concat_axis=0, tiled=True)


def flip(value, axis, bits):
    return lax.ppermute(value, axis, [(i, i ^ bits) for i in range(lax.axis_size(axis))])


def row_partials(chip_rows, weight, other_weight):
    chips = len(chip_rows)
    rows, hidden = chip_rows[0].shape
    shard = weight.shape[0]
    ys = lax.axis_size("y")
    inner = rows // ys

    def kernel(place, *refs):
        row_refs, (weight_ref, other_ref, out_ref, stack_ref, both) = refs[:chips], refs[chips:]
        chip, core = place[0], place[1]
        both[pl.ds(pl.multiple_of(core * shard, shard), shard)] = weight_ref[...]
        both[pl.ds(pl.multiple_of((1 - core) * shard, shard), shard)] = other_ref[...]
        for k in range(chips):
            owner = jnp.bitwise_xor(chip, k)
            block = row_refs[k][...]
            stack_ref[owner] = block
            part = lax.dot_general(
                block, both[...], (((1,), (1,)), ((), ())), preferred_element_type=jnp.float32
            ).astype(jnp.bfloat16)
            for y in range(ys):
                out_ref[y, owner] = part[y * inner : (y + 1) * inner]

    place = jnp.stack([lax.axis_index("xl"), lax.axis_index("core")]).astype(jnp.int32)
    return pl.pallas_call(
        kernel,
        out_shape=(
            jax.ShapeDtypeStruct((ys, chips, inner, 2 * shard), jnp.bfloat16),
            jax.ShapeDtypeStruct((chips, rows, hidden), jnp.bfloat16),
        ),
        in_specs=[pl.BlockSpec(memory_space=pltpu.SMEM)]
        + [pl.BlockSpec(memory_space=pltpu.VMEM)] * (chips + 2),
        out_specs=(pl.BlockSpec(memory_space=pltpu.VMEM),) * 2,
        scratch_shapes=[pltpu.VMEM((2 * shard, hidden), jnp.bfloat16)],
        compiler_params=pltpu.CompilerParams(vmem_limit_bytes=VMEM_BYTES),
        cost_estimate=pl.CostEstimate(
            flops=4 * chips * rows * hidden * shard, bytes_accessed=6 << 20, transcendentals=0
        ),
        name="row_partials",
    )(place, *chip_rows, weight, other_weight)


def weight_gradient(pieces, chip_rows, other_rows):
    chips, rows, hidden = chip_rows.shape
    ys = lax.axis_size("y")
    inner = rows // ys
    shard = pieces[0].shape[1]

    def kernel(place, *refs):
        piece_refs, (own_ref, other_ref, out_ref, layer) = refs[: len(pieces)], refs[len(pieces) :]
        core, here, beside = place[0], place[1], place[2]
        owners = (here, here ^ 4, here ^ 2, here ^ 6, here ^ 1, here ^ 5, beside, beside ^ 4)
        step = 0
        for ref in piece_refs:
            for half in range(ref.shape[0] // rows):
                for chip in range(chips):
                    for c in range(2):
                        start = half * rows + (chip * 2 + c) * inner
                        layer[jnp.bitwise_xor(core, c), chip, owners[step]] = ref[
                            start : start + inner
                        ]
                step += 1
        contract = (((0,), (0,)), ((), ()))
        for n in range(0, hidden, 256):
            total = jnp.zeros((shard, 256), jnp.float32)
            for side, ref in enumerate((own_ref, other_ref)):
                total += lax.dot_general(
                    layer[side].reshape(chips * rows, shard),
                    ref[:, :, n : n + 256].reshape(chips * rows, 256),
                    contract,
                    preferred_element_type=jnp.float32,
                )
            out_ref[:, n : n + 256] = total.astype(jnp.bfloat16)

    y = lax.axis_index("y")
    beside = (y + 1 + (ys - 2) * (1 - (y & 1))) & (ys - 1)
    place = jnp.stack([lax.axis_index("core"), y, beside]).astype(jnp.int32)
    return pl.pallas_call(
        kernel,
        out_shape=jax.ShapeDtypeStruct((shard, hidden), jnp.bfloat16),
        in_specs=[pl.BlockSpec(memory_space=pltpu.SMEM)]
        + [pl.BlockSpec(memory_space=pltpu.VMEM)] * (len(pieces) + 2),
        out_specs=pl.BlockSpec(memory_space=pltpu.VMEM),
        scratch_shapes=[pltpu.VMEM((2, chips, ys, inner, shard), jnp.bfloat16)],
        compiler_params=pltpu.CompilerParams(vmem_limit_bytes=VMEM_BYTES),
        cost_estimate=pl.CostEstimate(
            flops=4 * chips * rows * hidden * shard, bytes_accessed=6 << 20, transcendentals=0
        ),
        name="weight_gradient",
    )(place, *pieces, chip_rows, other_rows)


def on_device(tokens, routes, up_weight, hidden_grad, gate_pre):
    chips, cores, experts = lax.axis_size("xl"), lax.axis_size("core"), lax.axis_size("ex")
    ys, halves = lax.axis_size("y"), lax.axis_size("h")
    owners = chips * cores
    token_count, width = tokens.shape
    _, shard, hidden = up_weight.shape
    rows = hidden_grad.shape[1]
    inner = halves * experts

    grad_up = derive(hidden_grad[0], gate_pre[0])
    grad_up = grad_up.reshape(experts, ys, halves, hidden).transpose(1, 2, 0, 3)
    grad_up = grad_up.reshape(rows, hidden)
    far, farther, near = (flip(grad_up, "xl", k) for k in (2, 3, 1))
    weight = up_weight[0]
    other_weight = lax.ppermute(weight, "core", CORE_SWAP)

    picks = jnp.any(
        routes[:, :, None] == jnp.arange(experts, dtype=jnp.int32)[None, None, :], axis=1
    ).astype(jnp.bfloat16)
    outgoing = jnp.einsum(
        "te,tqc->qec",
        picks,
        tokens.reshape(token_count, owners, shard),
        preferred_element_type=jnp.float32,
    ).astype(jnp.bfloat16)
    outgoing = jnp.broadcast_to(outgoing[:, None], (owners, halves, experts, shard))
    arrived = exchange(
        outgoing.reshape(owners * halves, experts, shard), ("xl", "core", "h")
    )
    arrived = exchange(arrived.transpose(1, 0, 2), "ex")
    arrived = arrived.reshape(experts, owners, halves, shard).transpose(1, 2, 0, 3)
    arrived = arrived.reshape(rows, shard)

    partial, chip_rows = row_partials((grad_up, near, far, farther), weight, other_weight)
    summed = exchange(
        partial.reshape(ys * chips * halves, experts, cores * shard), ("y", "xl", "h")
    )
    summed = summed.reshape(ys, chips, halves, experts, cores * shard).astype(jnp.float32)
    row_grad = jnp.sum(summed, axis=(0, 2)).astype(jnp.bfloat16)
    returned = exchange(row_grad.transpose(1, 0, 2), "ex")
    grad_tokens = jnp.einsum(
        "te,eqc->tqc", picks, returned, preferred_element_type=jnp.float32
    ).astype(jnp.bfloat16)

    across = flip(arrived, "y", 4)
    pair = jnp.concatenate([arrived, across], axis=0)
    beside = [(y, (y + (ys - 1 if y % 2 == 0 else 1)) % ys) for y in range(ys)]
    pieces = (
        arrived,
        across,
        flip(pair, "y", 2),
        flip(pair, "y", 1),
        lax.ppermute(pair, "y", beside),
    )
    other_chip_rows = lax.ppermute(chip_rows, "core", CORE_SWAP)
    weight_grad = weight_gradient(pieces, chip_rows, other_chip_rows)
    return grad_tokens.reshape(token_count, width), weight_grad[None]


def solution(mesh):
    shape = (mesh.shape["dp"] // 2, 2, mesh.shape["expert"], mesh.shape["etensor"] // 2, 2)
    fine = Mesh(mesh.devices.reshape(shape), ("xl", "core", "ex", "y", "h"))
    tokens_spec = P(("xl", "core", "ex", "y", "h"), None)
    expert_spec = P("ex", ("xl", "core"), ("y", "h"))
    return jax.shard_map(
        on_device,
        mesh=fine,
        in_specs=(tokens_spec, tokens_spec, expert_spec, expert_spec, expert_spec),
        out_specs=(tokens_spec, expert_spec),
        check_vma=False,
    )
```

```python
import jax
import jax.numpy as jnp
from jax import lax
from jax.experimental import pallas as pl
from jax.experimental.pallas import tpu as pltpu
from jax.sharding import Mesh, PartitionSpec as P

CORE_SWAP = ((0, 1), (1, 0))
VMEM_BYTES = 40 * 1024 * 1024


def derive(grad_rows, gate_rows):
    gate_wide = gate_rows.astype(jnp.float32)
    sigma = jax.nn.sigmoid(gate_wide)
    return (grad_rows.astype(jnp.float32) * gate_wide * sigma).astype(jnp.bfloat16)


def exchange(blocks, axes):
    return lax.all_to_all(blocks, axes, split_axis=0, concat_axis=0, tiled=True)


def flip(value, axis, bits):
    return lax.ppermute(value, axis, [(i, i ^ bits) for i in range(lax.axis_size(axis))])


def place_of(*indices):
    return jnp.stack(indices).astype(jnp.int32)


SMEM = pl.BlockSpec(memory_space=pltpu.SMEM)
VMEM = pl.BlockSpec(memory_space=pltpu.VMEM)


def row_partials(chip_rows, weight, other_weight):
    chips = len(chip_rows)
    rows, hidden = chip_rows[0].shape
    shard = weight.shape[0]
    ys = lax.axis_size("y")
    inner = rows // ys

    def kernel(place, *refs):
        row_refs, (weight_ref, other_ref, out_ref, stack_ref) = refs[:chips], refs[chips:]
        chip, core = place[0], place[1]
        for k in range(chips):
            stack_ref[chip ^ k] = row_refs[k][...]
        blocks = stack_ref[...].reshape(chips * rows, hidden)
        for side, ref in ((core, weight_ref), (1 - core, other_ref)):
            part = lax.dot_general(
                blocks, ref[...], (((1,), (1,)), ((), ())), preferred_element_type=jnp.float32
            ).astype(jnp.bfloat16)
            columns = pl.ds(pl.multiple_of(side * shard, 128), shard)
            for chip_to in range(chips):
                for y in range(ys):
                    start = (chip_to * ys + y) * inner
                    out_ref[y, chip_to, :, columns] = part[start : start + inner]

    return pl.pallas_call(
        kernel,
        out_shape=(
            jax.ShapeDtypeStruct((ys, chips, inner, 2 * shard), jnp.bfloat16),
            jax.ShapeDtypeStruct((chips, rows, hidden), jnp.bfloat16),
        ),
        in_specs=[SMEM] + [VMEM] * (chips + 2),
        out_specs=(VMEM,) * 2,
        compiler_params=pltpu.CompilerParams(vmem_limit_bytes=VMEM_BYTES),
        cost_estimate=pl.CostEstimate(
            flops=4 * chips * rows * hidden * shard, bytes_accessed=6 << 20, transcendentals=0
        ),
        name="row_partials",
    )(
        place_of(lax.axis_index("xl"), lax.axis_index("core")),
        *chip_rows, weight, other_weight,
    )


def reduce_rows(partials):
    ys, chips, halves, experts, features = partials.shape

    def kernel(in_ref, out_ref):
        sums = []
        for chip in range(chips):
            total = jnp.zeros((experts, features), jnp.float32)
            for y in range(ys):
                for half in range(halves):
                    total += in_ref[y, chip, half].astype(jnp.float32)
            sums.append(total)
        out_ref[...] = jnp.stack(sums, axis=1).astype(jnp.bfloat16)

    return pl.pallas_call(
        kernel,
        out_shape=jax.ShapeDtypeStruct((experts, chips, features), jnp.bfloat16),
        in_specs=[VMEM],
        out_specs=VMEM,
        compiler_params=pltpu.CompilerParams(vmem_limit_bytes=VMEM_BYTES),
        cost_estimate=pl.CostEstimate(
            flops=ys * halves * chips * experts * features, bytes_accessed=1 << 20, transcendentals=0
        ),
        name="reduce_rows",
    )(partials)


def weight_gradient(token_rows, chip_rows, other_rows):
    chips, rows, hidden = chip_rows.shape
    ys, _, shard = token_rows.shape
    inner = rows // ys

    def kernel(place, token_ref, own_ref, other_ref, out_ref, layer):
        core = place[0]
        for y in range(ys):
            for chip in range(chips):
                for c in range(2):
                    start = (chip * 2 + c) * inner
                    layer[core ^ c, chip, y] = token_ref[y, start : start + inner]
        contract = (((0,), (0,)), ((), ()))
        for n in range(0, hidden, 256):
            total = jnp.zeros((shard, 256), jnp.float32)
            for side, ref in enumerate((own_ref, other_ref)):
                total += lax.dot_general(
                    layer[side].reshape(chips * rows, shard),
                    ref[:, :, n : n + 256].reshape(chips * rows, 256),
                    contract,
                    preferred_element_type=jnp.float32,
                )
            out_ref[:, n : n + 256] = total.astype(jnp.bfloat16)

    return pl.pallas_call(
        kernel,
        out_shape=jax.ShapeDtypeStruct((shard, hidden), jnp.bfloat16),
        in_specs=[SMEM] + [VMEM] * 3,
        out_specs=VMEM,
        scratch_shapes=[pltpu.VMEM((2, chips, ys, inner, shard), jnp.bfloat16)],
        compiler_params=pltpu.CompilerParams(vmem_limit_bytes=VMEM_BYTES),
        cost_estimate=pl.CostEstimate(
            flops=4 * chips * rows * hidden * shard, bytes_accessed=6 << 20, transcendentals=0
        ),
        name="weight_gradient",
    )(place_of(lax.axis_index("core")), token_rows, chip_rows, other_rows)


def on_device(tokens, routes, up_weight, hidden_grad, gate_pre):
    chips, cores, experts = lax.axis_size("xl"), lax.axis_size("core"), lax.axis_size("ex")
    ys, halves = lax.axis_size("y"), lax.axis_size("h")
    owners = chips * cores
    token_count, width = tokens.shape
    _, shard, hidden = up_weight.shape
    rows = hidden_grad.shape[1]
    inner = halves * experts

    grad_up = derive(hidden_grad[0], gate_pre[0])
    grad_up = grad_up.reshape(experts, ys, halves, hidden).transpose(1, 2, 0, 3)
    grad_up = grad_up.reshape(rows, hidden)
    far, farther, near = (flip(grad_up, "xl", k) for k in (2, 3, 1))

    picks = jnp.any(
        routes[:, :, None] == jnp.arange(experts, dtype=jnp.int32)[None, None, :], axis=1
    ).astype(jnp.bfloat16)
    outgoing = jnp.einsum(
        "te,tqc->qec",
        picks,
        tokens.reshape(token_count, owners, shard),
        preferred_element_type=jnp.float32,
    ).astype(jnp.bfloat16)
    outgoing = jnp.broadcast_to(outgoing[:, None], (owners, halves, experts, shard))
    arrived = exchange(
        outgoing.reshape(owners * halves, experts, shard), ("xl", "core", "h")
    )
    arrived, weight = lax.optimization_barrier((arrived, up_weight[0]))
    other_weight = lax.ppermute(weight, "core", CORE_SWAP)
    arrived = exchange(arrived.transpose(1, 0, 2), "ex")
    arrived = arrived.reshape(experts, owners, halves, shard).transpose(1, 2, 0, 3)
    arrived = arrived.reshape(rows, shard)

    arrived, near, far = lax.optimization_barrier((arrived, near, far))
    token_rows = exchange(jnp.broadcast_to(arrived[None], (ys,) + arrived.shape), "y")

    partial, chip_rows = row_partials(
        (grad_up, near, far, farther), weight, other_weight
    )
    partial, token_rows = lax.optimization_barrier((partial, token_rows))
    partial = exchange(
        partial.reshape(ys * chips * halves, experts, cores * shard), ("y", "xl", "h")
    )
    row_grad = reduce_rows(partial.reshape(ys, chips, halves, experts, cores * shard))
    returned = exchange(row_grad, "ex")
    grad_tokens = jnp.einsum(
        "te,eqc->tqc", picks, returned, preferred_element_type=jnp.float32
    ).astype(jnp.bfloat16)

    other_chip_rows = lax.ppermute(chip_rows, "core", CORE_SWAP)
    weight_grad = weight_gradient(token_rows, chip_rows, other_chip_rows)
    return grad_tokens.reshape(token_count, width), weight_grad[None]


def solution(mesh):
    shape = (mesh.shape["dp"] // 2, 2, mesh.shape["expert"], mesh.shape["etensor"] // 2, 2)
    fine = Mesh(mesh.devices.reshape(shape), ("xl", "core", "ex", "y", "h"))
    tokens_spec = P(("xl", "core", "ex", "y", "h"), None)
    expert_spec = P("ex", ("xl", "core"), ("y", "h"))
    return jax.shard_map(
        on_device,
        mesh=fine,
        in_specs=(tokens_spec, tokens_spec, expert_spec, expert_spec, expert_spec),
        out_specs=(tokens_spec, expert_spec),
        check_vma=False,
    )
```

```python
import jax
import jax.numpy as jnp
from jax import lax
from jax.experimental import pallas as pl
from jax.experimental.pallas import tpu as pltpu
from jax.sharding import Mesh, PartitionSpec as P

CORE_SWAP = ((0, 1), (1, 0))
VMEM_BYTES = 40 * 1024 * 1024


def derive(grad_rows, gate_rows):
    gate_wide = gate_rows.astype(jnp.float32)
    sigma = jax.nn.sigmoid(gate_wide)
    return (grad_rows.astype(jnp.float32) * gate_wide * sigma).astype(jnp.bfloat16)


def exchange(blocks, axes):
    return lax.all_to_all(blocks, axes, split_axis=0, concat_axis=0, tiled=True)


def flip(value, axis, bits):
    return lax.ppermute(value, axis, [(i, i ^ bits) for i in range(lax.axis_size(axis))])


def shift(value, axis, by):
    size = lax.axis_size(axis)
    return lax.ppermute(value, axis, [(i, (i + by) % size) for i in range(size)])


def place_of(*indices):
    return jnp.stack(indices).astype(jnp.int32)


SMEM = pl.BlockSpec(memory_space=pltpu.SMEM)
VMEM = pl.BlockSpec(memory_space=pltpu.VMEM)


def row_partials(chip_rows, weight, other_weight):
    chips = len(chip_rows)
    rows, hidden = chip_rows[0].shape
    shard = weight.shape[0]
    ys = lax.axis_size("yh") * lax.axis_size("yl")
    inner = rows // ys

    def kernel(place, *refs):
        row_refs, (weight_ref, other_ref, out_ref, stack_ref) = refs[:chips], refs[chips:]
        chip, core = place[0], place[1]
        for k in range(chips):
            stack_ref[chip ^ k] = row_refs[k][...]
        blocks = stack_ref[...].reshape(chips * rows, hidden)
        for side, ref in ((core, weight_ref), (1 - core, other_ref)):
            part = lax.dot_general(
                blocks, ref[...], (((1,), (1,)), ((), ())), preferred_element_type=jnp.float32
            ).astype(jnp.bfloat16)
            columns = pl.ds(pl.multiple_of(side * shard, 128), shard)
            for chip_to in range(chips):
                for y in range(ys):
                    start = (chip_to * ys + y) * inner
                    out_ref[y, chip_to, :, columns] = part[start : start + inner]

    return pl.pallas_call(
        kernel,
        out_shape=(
            jax.ShapeDtypeStruct((ys, chips, inner, 2 * shard), jnp.bfloat16),
            jax.ShapeDtypeStruct((chips, rows, hidden), jnp.bfloat16),
        ),
        in_specs=[SMEM] + [VMEM] * (chips + 2),
        out_specs=(VMEM,) * 2,
        compiler_params=pltpu.CompilerParams(vmem_limit_bytes=VMEM_BYTES),
        cost_estimate=pl.CostEstimate(
            flops=64 * chips * rows * hidden * shard, bytes_accessed=6 << 20, transcendentals=0
        ),
        name="row_partials",
    )(
        place_of(lax.axis_index("xl"), lax.axis_index("core")),
        *chip_rows, weight, other_weight,
    )


def reduce_rows(partials):
    ys, chips, halves, experts, features = partials.shape

    def kernel(in_ref, out_ref):
        sums = []
        for chip in range(chips):
            total = jnp.zeros((experts, features), jnp.float32)
            for y in range(ys):
                for half in range(halves):
                    total += in_ref[y, chip, half].astype(jnp.float32)
            sums.append(total)
        out_ref[...] = jnp.stack(sums, axis=1).astype(jnp.bfloat16)

    return pl.pallas_call(
        kernel,
        out_shape=jax.ShapeDtypeStruct((experts, chips, features), jnp.bfloat16),
        in_specs=[VMEM],
        out_specs=VMEM,
        compiler_params=pltpu.CompilerParams(vmem_limit_bytes=VMEM_BYTES),
        cost_estimate=pl.CostEstimate(
            flops=ys * halves * chips * experts * features, bytes_accessed=1 << 20, transcendentals=0
        ),
        name="reduce_rows",
    )(partials)


def weight_gradient(pieces, chip_rows, other_rows):
    chips, rows, hidden = chip_rows.shape
    twins, shard = pieces[0].shape[0] // rows, pieces[0].shape[1]
    ys = len(pieces) * twins
    inner = rows // ys

    def kernel(place, *refs):
        piece_refs, (own_ref, other_ref, out_ref, layer) = refs[: len(pieces)], refs[len(pieces) :]
        core, pair = place[0], place[1]
        for away, ref in enumerate(piece_refs):
            for twin in range(twins):
                y = ((pair + away) & (len(pieces) - 1)) * twins + twin
                for chip in range(chips):
                    for c in range(2):
                        start = twin * rows + (chip * 2 + c) * inner
                        layer[core ^ c, chip, y] = ref[start : start + inner]
        contract = (((0,), (0,)), ((), ()))
        for n in range(0, hidden, 256):
            total = jnp.zeros((shard, 256), jnp.float32)
            for side, ref in enumerate((own_ref, other_ref)):
                total += lax.dot_general(
                    layer[side].reshape(chips * rows, shard),
                    ref[:, :, n : n + 256].reshape(chips * rows, 256),
                    contract,
                    preferred_element_type=jnp.float32,
                )
            out_ref[:, n : n + 256] = total.astype(jnp.bfloat16)

    return pl.pallas_call(
        kernel,
        out_shape=jax.ShapeDtypeStruct((shard, hidden), jnp.bfloat16),
        in_specs=[SMEM] + [VMEM] * (len(pieces) + 2),
        out_specs=VMEM,
        scratch_shapes=[pltpu.VMEM((2, chips, ys, inner, shard), jnp.bfloat16)],
        compiler_params=pltpu.CompilerParams(vmem_limit_bytes=VMEM_BYTES),
        cost_estimate=pl.CostEstimate(
            flops=4 * chips * rows * hidden * shard, bytes_accessed=6 << 20, transcendentals=0
        ),
        name="weight_gradient",
    )(place_of(lax.axis_index("core"), lax.axis_index("yh")), *pieces, chip_rows, other_rows)


def on_device(tokens, routes, up_weight, hidden_grad, gate_pre):
    chips, cores, experts = lax.axis_size("xl"), lax.axis_size("core"), lax.axis_size("ex")
    pairs, twins = lax.axis_size("yh"), lax.axis_size("yl")
    ys, halves = pairs * twins, lax.axis_size("h")
    owners = chips * cores
    token_count, width = tokens.shape
    _, shard, hidden = up_weight.shape
    rows = hidden_grad.shape[1]
    inner = halves * experts

    grad_up = derive(hidden_grad[0], gate_pre[0])
    grad_up = grad_up.reshape(experts, ys, halves, hidden).transpose(1, 2, 0, 3)
    grad_up = grad_up.reshape(rows, hidden)
    far, farther, near = (flip(grad_up, "xl", k) for k in (2, 3, 1))

    picks = jnp.any(
        routes[:, :, None] == jnp.arange(experts, dtype=jnp.int32)[None, None, :], axis=1
    ).astype(jnp.bfloat16)
    outgoing = jnp.einsum(
        "te,tqc->qec",
        picks,
        tokens.reshape(token_count, owners, shard),
        preferred_element_type=jnp.float32,
    ).astype(jnp.bfloat16)
    outgoing = jnp.broadcast_to(outgoing[:, None], (owners, halves, experts, shard))
    arrived = exchange(
        outgoing.reshape(owners * halves, experts, shard), ("xl", "core", "h")
    )
    weight = up_weight[0]
    other_weight = lax.ppermute(weight, "core", CORE_SWAP)
    arrived = jnp.broadcast_to(
        arrived.transpose(1, 0, 2)[:, None], (experts, twins, owners * halves, shard)
    )
    arrived = exchange(
        arrived.reshape(experts * twins, owners * halves, shard), ("ex", "yl")
    )
    arrived = arrived.reshape(experts, twins, owners, halves, shard).transpose(1, 2, 3, 0, 4)
    arrived = arrived.reshape(twins * rows, shard)

    partial, chip_rows = row_partials(
        (grad_up, near, far, farther), weight, other_weight
    )
    partial = exchange(
        partial.reshape(ys * chips * halves, experts, cores * shard), ("yh", "yl", "xl", "h")
    )
    row_grad = reduce_rows(partial.reshape(ys, chips, halves, experts, cores * shard))
    returned = exchange(row_grad, "ex")
    grad_tokens = jnp.einsum(
        "te,eqc->tqc", picks, returned, preferred_element_type=jnp.float32
    ).astype(jnp.bfloat16)

    pieces = [arrived] + [shift(arrived, "yh", -away) for away in range(1, pairs)]
    other_chip_rows = lax.ppermute(chip_rows, "core", CORE_SWAP)
    weight_grad = weight_gradient(pieces, chip_rows, other_chip_rows)
    return grad_tokens.reshape(token_count, width), weight_grad[None]


def solution(mesh):
    shape = (mesh.shape["dp"] // 2, 2, mesh.shape["expert"], mesh.shape["etensor"] // 4, 2, 2)
    fine = Mesh(mesh.devices.reshape(shape), ("xl", "core", "ex", "yh", "yl", "h"))
    tokens_spec = P(("xl", "core", "ex", "yh", "yl", "h"), None)
    expert_spec = P("ex", ("xl", "core"), ("yh", "yl", "h"))
    return jax.shard_map(
        on_device,
        mesh=fine,
        in_specs=(tokens_spec, tokens_spec, expert_spec, expert_spec, expert_spec),
        out_specs=(tokens_spec, expert_spec),
        check_vma=False,
    )
```

```python
import jax
import jax.numpy as jnp
from jax import lax
from jax.experimental import pallas as pl
from jax.experimental.pallas import tpu as pltpu
from jax.sharding import Mesh, PartitionSpec as P

CORE_SWAP = ((0, 1), (1, 0))
VMEM_BYTES = 40 * 1024 * 1024


def derive(grad_rows, gate_rows):
    gate_wide = gate_rows.astype(jnp.float32)
    sigma = jax.nn.sigmoid(gate_wide)
    return (grad_rows.astype(jnp.float32) * gate_wide * sigma).astype(jnp.bfloat16)


def exchange(blocks, axes):
    return lax.all_to_all(blocks, axes, split_axis=0, concat_axis=0, tiled=True)


def flip(value, axis, bits):
    return lax.ppermute(value, axis, [(i, i ^ bits) for i in range(lax.axis_size(axis))])


def shift(value, axis, by):
    size = lax.axis_size(axis)
    return lax.ppermute(value, axis, [(i, (i + by) % size) for i in range(size)])


def place_of(*indices):
    return jnp.stack(indices).astype(jnp.int32)


SMEM = pl.BlockSpec(memory_space=pltpu.SMEM)
VMEM = pl.BlockSpec(memory_space=pltpu.VMEM)


def row_partials(chip_rows, weight, other_weight):
    chips = len(chip_rows)
    rows, hidden = chip_rows[0].shape
    shard = weight.shape[0]
    ys = lax.axis_size("yh") * lax.axis_size("yl")
    inner = rows // ys

    def kernel(place, *refs):
        row_refs, (weight_ref, other_ref, out_ref, stack_ref) = refs[:chips], refs[chips:]
        chip, core = place[0], place[1]
        for k in range(chips):
            stack_ref[chip ^ k] = row_refs[k][...]
        blocks = stack_ref[...].reshape(chips * rows, hidden)
        for side, ref in ((core, weight_ref), (1 - core, other_ref)):
            part = lax.dot_general(
                blocks, ref[...], (((1,), (1,)), ((), ())), preferred_element_type=jnp.float32
            ).astype(jnp.bfloat16)
            columns = pl.ds(pl.multiple_of(side * shard, 128), shard)
            for chip_to in range(chips):
                for y in range(ys):
                    start = (chip_to * ys + y) * inner
                    out_ref[y, chip_to, :, columns] = part[start : start + inner]

    return pl.pallas_call(
        kernel,
        out_shape=(
            jax.ShapeDtypeStruct((ys, chips, inner, 2 * shard), jnp.bfloat16),
            jax.ShapeDtypeStruct((chips, rows, hidden), jnp.bfloat16),
        ),
        in_specs=[SMEM] + [VMEM] * (chips + 2),
        out_specs=(VMEM,) * 2,
        compiler_params=pltpu.CompilerParams(vmem_limit_bytes=VMEM_BYTES),
        cost_estimate=pl.CostEstimate(
            flops=8 * chips * rows * hidden * shard, bytes_accessed=6 << 20, transcendentals=0
        ),
        name="row_partials",
    )(
        place_of(lax.axis_index("xl"), lax.axis_index("core")),
        *chip_rows, weight, other_weight,
    )


def reduce_rows(partials):
    ys, chips, halves, experts, features = partials.shape

    def kernel(in_ref, out_ref):
        sums = []
        for chip in range(chips):
            total = jnp.zeros((experts, features), jnp.float32)
            for y in range(ys):
                for half in range(halves):
                    total += in_ref[y, chip, half].astype(jnp.float32)
            sums.append(total)
        out_ref[...] = jnp.stack(sums, axis=1).astype(jnp.bfloat16)

    return pl.pallas_call(
        kernel,
        out_shape=jax.ShapeDtypeStruct((experts, chips, features), jnp.bfloat16),
        in_specs=[VMEM],
        out_specs=VMEM,
        compiler_params=pltpu.CompilerParams(vmem_limit_bytes=VMEM_BYTES),
        cost_estimate=pl.CostEstimate(
            flops=ys * halves * chips * experts * features, bytes_accessed=1 << 20, transcendentals=0
        ),
        name="reduce_rows",
    )(partials)


def weight_gradient(pieces, chip_rows, other_rows):
    chips, rows, hidden = chip_rows.shape
    twins, shard = pieces[0].shape[0] // rows, pieces[0].shape[1]
    ys = len(pieces) * twins
    inner = rows // ys

    def kernel(place, *refs):
        piece_refs, (own_ref, other_ref, out_ref, layer) = refs[: len(pieces)], refs[len(pieces) :]
        core, pair = place[0], place[1]
        for away, ref in enumerate(piece_refs):
            for twin in range(twins):
                y = ((pair + away) & (len(pieces) - 1)) * twins + twin
                for chip in range(chips):
                    for c in range(2):
                        start = twin * rows + (chip * 2 + c) * inner
                        layer[core ^ c, chip, y] = ref[start : start + inner]
        contract = (((0,), (0,)), ((), ()))
        for n in range(0, hidden, 256):
            total = jnp.zeros((shard, 256), jnp.float32)
            for side, ref in enumerate((own_ref, other_ref)):
                total += lax.dot_general(
                    layer[side].reshape(chips * rows, shard),
                    ref[:, :, n : n + 256].reshape(chips * rows, 256),
                    contract,
                    preferred_element_type=jnp.float32,
                )
            out_ref[:, n : n + 256] = total.astype(jnp.bfloat16)

    return pl.pallas_call(
        kernel,
        out_shape=jax.ShapeDtypeStruct((shard, hidden), jnp.bfloat16),
        in_specs=[SMEM] + [VMEM] * (len(pieces) + 2),
        out_specs=VMEM,
        scratch_shapes=[pltpu.VMEM((2, chips, ys, inner, shard), jnp.bfloat16)],
        compiler_params=pltpu.CompilerParams(vmem_limit_bytes=VMEM_BYTES),
        cost_estimate=pl.CostEstimate(
            flops=4 * chips * rows * hidden * shard, bytes_accessed=6 << 20, transcendentals=0
        ),
        name="weight_gradient",
    )(place_of(lax.axis_index("core"), lax.axis_index("yh")), *pieces, chip_rows, other_rows)


def on_device(tokens, routes, up_weight, hidden_grad, gate_pre):
    chips, cores, experts = lax.axis_size("xl"), lax.axis_size("core"), lax.axis_size("ex")
    pairs, twins = lax.axis_size("yh"), lax.axis_size("yl")
    ys, halves = pairs * twins, lax.axis_size("h")
    owners = chips * cores
    token_count, width = tokens.shape
    _, shard, hidden = up_weight.shape
    rows = hidden_grad.shape[1]
    inner = halves * experts

    grad_up = derive(hidden_grad[0], gate_pre[0])
    grad_up = grad_up.reshape(experts, ys, halves, hidden).transpose(1, 2, 0, 3)
    grad_up = grad_up.reshape(rows, hidden)
    far, farther, near = (flip(grad_up, "xl", k) for k in (2, 3, 1))

    picks = jnp.any(
        routes[:, :, None] == jnp.arange(experts, dtype=jnp.int32)[None, None, :], axis=1
    ).astype(jnp.bfloat16)
    outgoing = jnp.einsum(
        "te,tqc->qec",
        picks,
        tokens.reshape(token_count, owners, shard),
        preferred_element_type=jnp.float32,
    ).astype(jnp.bfloat16)
    outgoing = jnp.broadcast_to(outgoing[:, None], (owners, halves, experts, shard))
    arrived = exchange(
        outgoing.reshape(owners * halves, experts, shard), ("xl", "core", "h")
    )
    weight = up_weight[0]
    other_weight = lax.ppermute(weight, "core", CORE_SWAP)
    arrived = jnp.broadcast_to(
        arrived.transpose(1, 0, 2)[:, None], (experts, twins, owners * halves, shard)
    )
    arrived = exchange(
        arrived.reshape(experts * twins, owners * halves, shard), ("ex", "yl")
    )
    arrived = arrived.reshape(experts, twins, owners, halves, shard).transpose(1, 2, 3, 0, 4)
    arrived = arrived.reshape(twins * rows, shard)

    partial, chip_rows = row_partials(
        (grad_up, near, far, farther), weight, other_weight
    )
    partial = exchange(
        partial.reshape(ys * chips * halves, experts, cores * shard), ("yh", "yl", "xl", "h")
    )
    row_grad = reduce_rows(partial.reshape(ys, chips, halves, experts, cores * shard))
    returned = exchange(row_grad, "ex")
    grad_tokens = jnp.einsum(
        "te,eqc->tqc", picks, returned, preferred_element_type=jnp.float32
    ).astype(jnp.bfloat16)

    pieces = [arrived] + [shift(arrived, "yh", -away) for away in range(1, pairs)]
    other_chip_rows = lax.ppermute(chip_rows, "core", CORE_SWAP)
    weight_grad = weight_gradient(pieces, chip_rows, other_chip_rows)
    return grad_tokens.reshape(token_count, width), weight_grad[None]


def solution(mesh):
    shape = (mesh.shape["dp"] // 2, 2, mesh.shape["expert"], mesh.shape["etensor"] // 4, 2, 2)
    fine = Mesh(mesh.devices.reshape(shape), ("xl", "core", "ex", "yh", "yl", "h"))
    tokens_spec = P(("xl", "core", "ex", "yh", "yl", "h"), None)
    expert_spec = P("ex", ("xl", "core"), ("yh", "yl", "h"))
    return jax.shard_map(
        on_device,
        mesh=fine,
        in_specs=(tokens_spec, tokens_spec, expert_spec, expert_spec, expert_spec),
        out_specs=(tokens_spec, expert_spec),
        check_vma=False,
    )
```

```python
import jax
import jax.numpy as jnp
from jax import lax
from jax.experimental import pallas as pl
from jax.experimental.pallas import tpu as pltpu
from jax.sharding import Mesh, PartitionSpec as P

CORE_SWAP = ((0, 1), (1, 0))
VMEM_BYTES = 40 * 1024 * 1024


def derive(grad_rows, gate_rows):
    gate_wide = gate_rows.astype(jnp.float32)
    sigma = jax.nn.sigmoid(gate_wide)
    return (grad_rows.astype(jnp.float32) * gate_wide * sigma).astype(jnp.bfloat16)


def exchange(blocks, axes):
    return lax.all_to_all(blocks, axes, split_axis=0, concat_axis=0, tiled=True)


def flip(value, axis, bits):
    return lax.ppermute(value, axis, [(i, i ^ bits) for i in range(lax.axis_size(axis))])


def shift(value, axis, by):
    size = lax.axis_size(axis)
    return lax.ppermute(value, axis, [(i, (i + by) % size) for i in range(size)])


def place_of(*indices):
    return jnp.stack(indices).astype(jnp.int32)


SMEM = pl.BlockSpec(memory_space=pltpu.SMEM)
VMEM = pl.BlockSpec(memory_space=pltpu.VMEM)


def row_partials(chip_rows, weight, other_weight):
    chips = lax.axis_size("xl")
    rows, hidden = chip_rows[0].shape
    shard = weight.shape[0]
    ys = lax.axis_size("yh") * lax.axis_size("yl")
    inner = rows // ys

    def kernel(place, *refs):
        own, near, opposite, across, forwarded = refs[:5]
        weight_ref, other_ref, out_ref, stack_ref = refs[5:]
        chip, core = place[0], place[1]
        middle = jnp.logical_and(chip > 0, chip < chips - 1)
        stack_ref[chip] = own[...]
        stack_ref[chip ^ 1] = near[...]
        stack_ref[chip ^ 3] = opposite[...]

        @pl.when(middle)
        def _():
            stack_ref[chip ^ 2] = across[...]

        @pl.when(jnp.logical_not(middle))
        def _():
            stack_ref[chip ^ 2] = forwarded[...]

        blocks = stack_ref[...].reshape(chips * rows, hidden)
        for side, ref in ((core, weight_ref), (1 - core, other_ref)):
            part = lax.dot_general(
                blocks, ref[...], (((1,), (1,)), ((), ())), preferred_element_type=jnp.float32
            ).astype(jnp.bfloat16)
            columns = pl.ds(pl.multiple_of(side * shard, 128), shard)
            for chip_to in range(chips):
                for y in range(ys):
                    start = (chip_to * ys + y) * inner
                    out_ref[y, chip_to, :, columns] = part[start : start + inner]

    return pl.pallas_call(
        kernel,
        out_shape=(
            jax.ShapeDtypeStruct((ys, chips, inner, 2 * shard), jnp.bfloat16),
            jax.ShapeDtypeStruct((chips, rows, hidden), jnp.bfloat16),
        ),
        in_specs=[SMEM] + [VMEM] * (len(chip_rows) + 2),
        out_specs=(VMEM,) * 2,
        compiler_params=pltpu.CompilerParams(vmem_limit_bytes=VMEM_BYTES),
        cost_estimate=pl.CostEstimate(
            flops=8 * chips * rows * hidden * shard, bytes_accessed=6 << 20, transcendentals=0
        ),
        name="row_partials",
    )(
        place_of(lax.axis_index("xl"), lax.axis_index("core")),
        *chip_rows, weight, other_weight,
    )


def reduce_rows(partials):
    ys, chips, halves, experts, features = partials.shape

    def kernel(in_ref, out_ref):
        sums = []
        for chip in range(chips):
            total = jnp.zeros((experts, features), jnp.float32)
            for y in range(ys):
                for half in range(halves):
                    total += in_ref[y, chip, half].astype(jnp.float32)
            sums.append(total)
        out_ref[...] = jnp.stack(sums, axis=1).astype(jnp.bfloat16)

    return pl.pallas_call(
        kernel,
        out_shape=jax.ShapeDtypeStruct((experts, chips, features), jnp.bfloat16),
        in_specs=[VMEM],
        out_specs=VMEM,
        compiler_params=pltpu.CompilerParams(vmem_limit_bytes=VMEM_BYTES),
        cost_estimate=pl.CostEstimate(
            flops=ys * halves * chips * experts * features, bytes_accessed=1 << 20, transcendentals=0
        ),
        name="reduce_rows",
    )(partials)


def weight_gradient(pieces, chip_rows, other_rows):
    chips, rows, hidden = chip_rows.shape
    twins, shard = pieces[0].shape[0] // rows, pieces[0].shape[1]
    ys = len(pieces) * twins
    inner = rows // ys

    def kernel(place, *refs):
        piece_refs, (own_ref, other_ref, out_ref, layer) = refs[: len(pieces)], refs[len(pieces) :]
        core, pair = place[0], place[1]
        for away, ref in enumerate(piece_refs):
            for twin in range(twins):
                y = ((pair + away) & (len(pieces) - 1)) * twins + twin
                for chip in range(chips):
                    for c in range(2):
                        start = twin * rows + (chip * 2 + c) * inner
                        layer[core ^ c, chip, y] = ref[start : start + inner]
        contract = (((0,), (0,)), ((), ()))
        for n in range(0, hidden, 256):
            total = jnp.zeros((shard, 256), jnp.float32)
            for side, ref in enumerate((own_ref, other_ref)):
                total += lax.dot_general(
                    layer[side].reshape(chips * rows, shard),
                    ref[:, :, n : n + 256].reshape(chips * rows, 256),
                    contract,
                    preferred_element_type=jnp.float32,
                )
            out_ref[:, n : n + 256] = total.astype(jnp.bfloat16)

    return pl.pallas_call(
        kernel,
        out_shape=jax.ShapeDtypeStruct((shard, hidden), jnp.bfloat16),
        in_specs=[SMEM] + [VMEM] * (len(pieces) + 2),
        out_specs=VMEM,
        scratch_shapes=[pltpu.VMEM((2, chips, ys, inner, shard), jnp.bfloat16)],
        compiler_params=pltpu.CompilerParams(vmem_limit_bytes=VMEM_BYTES),
        cost_estimate=pl.CostEstimate(
            flops=4 * chips * rows * hidden * shard, bytes_accessed=6 << 20, transcendentals=0
        ),
        name="weight_gradient",
    )(place_of(lax.axis_index("core"), lax.axis_index("yh")), *pieces, chip_rows, other_rows)


def on_device(tokens, routes, up_weight, hidden_grad, gate_pre):
    chips, cores, experts = lax.axis_size("xl"), lax.axis_size("core"), lax.axis_size("ex")
    pairs, twins = lax.axis_size("yh"), lax.axis_size("yl")
    ys, halves = pairs * twins, lax.axis_size("h")
    owners = chips * cores
    token_count, width = tokens.shape
    _, shard, hidden = up_weight.shape
    rows = hidden_grad.shape[1]
    inner = halves * experts

    grad_up = derive(hidden_grad[0], gate_pre[0])
    grad_up = grad_up.reshape(experts, ys, halves, hidden).transpose(1, 2, 0, 3)
    grad_up = grad_up.reshape(rows, hidden)
    opposite = flip(grad_up, "xl", 3)
    across = lax.ppermute(grad_up, "xl", [(0, 2), (3, 1)])
    near = flip(grad_up, "xl", 1)
    forwarded = lax.ppermute(opposite, "xl", [(2, 3), (1, 0)])

    picks = jnp.any(
        routes[:, :, None] == jnp.arange(experts, dtype=jnp.int32)[None, None, :], axis=1
    ).astype(jnp.bfloat16)
    outgoing = jnp.einsum(
        "te,tqc->qec",
        picks,
        tokens.reshape(token_count, owners, shard),
        preferred_element_type=jnp.float32,
    ).astype(jnp.bfloat16)
    outgoing = jnp.broadcast_to(outgoing[:, None], (owners, halves, experts, shard))
    arrived = exchange(
        outgoing.reshape(owners * halves, experts, shard), ("xl", "core", "h")
    )
    weight = up_weight[0]
    other_weight = lax.ppermute(weight, "core", CORE_SWAP)
    arrived = jnp.broadcast_to(
        arrived.transpose(1, 0, 2)[:, None], (experts, twins, owners * halves, shard)
    )
    arrived = exchange(
        arrived.reshape(experts * twins, owners * halves, shard), ("ex", "yl")
    )
    arrived = arrived.reshape(experts, twins, owners, halves, shard).transpose(1, 2, 3, 0, 4)
    arrived = arrived.reshape(twins * rows, shard)

    partial, chip_rows = row_partials(
        (grad_up, near, opposite, across, forwarded), weight, other_weight
    )
    partial = exchange(
        partial.reshape(ys * chips * halves, experts, cores * shard), ("yh", "yl", "xl", "h")
    )
    row_grad = reduce_rows(partial.reshape(ys, chips, halves, experts, cores * shard))
    returned = exchange(row_grad, "ex")
    grad_tokens = jnp.einsum(
        "te,eqc->tqc", picks, returned, preferred_element_type=jnp.float32
    ).astype(jnp.bfloat16)

    facing = shift(arrived, "yh", pairs // 2)
    pieces = [arrived, shift(arrived, "yh", -1), facing, shift(arrived, "yh", 1)]
    other_chip_rows = lax.ppermute(chip_rows, "core", CORE_SWAP)
    weight_grad = weight_gradient(pieces, chip_rows, other_chip_rows)
    return grad_tokens.reshape(token_count, width), weight_grad[None]


def solution(mesh):
    shape = (mesh.shape["dp"] // 2, 2, mesh.shape["expert"], mesh.shape["etensor"] // 4, 2, 2)
    fine = Mesh(mesh.devices.reshape(shape), ("xl", "core", "ex", "yh", "yl", "h"))
    tokens_spec = P(("xl", "core", "ex", "yh", "yl", "h"), None)
    expert_spec = P("ex", ("xl", "core"), ("yh", "yl", "h"))
    return jax.shard_map(
        on_device,
        mesh=fine,
        in_specs=(tokens_spec, tokens_spec, expert_spec, expert_spec, expert_spec),
        out_specs=(tokens_spec, expert_spec),
        check_vma=False,
    )
```

```python
import jax
import jax.numpy as jnp
from jax import lax
from jax.experimental import pallas as pl
from jax.experimental.pallas import tpu as pltpu
from jax.sharding import Mesh, PartitionSpec as P

CORE_SWAP = ((0, 1), (1, 0))
VMEM_BYTES = 40 * 1024 * 1024


def derive(grad_rows, gate_rows):
    gate_wide = gate_rows.astype(jnp.float32)
    sigma = jax.nn.sigmoid(gate_wide)
    return (grad_rows.astype(jnp.float32) * gate_wide * sigma).astype(jnp.bfloat16)


def exchange(blocks, axes):
    return lax.all_to_all(blocks, axes, split_axis=0, concat_axis=0, tiled=True)


def flip(value, axis, bits):
    return lax.ppermute(value, axis, [(i, i ^ bits) for i in range(lax.axis_size(axis))])


def shift(value, axis, by):
    size = lax.axis_size(axis)
    return lax.ppermute(value, axis, [(i, (i + by) % size) for i in range(size)])


def place_of(*indices):
    return jnp.stack(indices).astype(jnp.int32)


SMEM = pl.BlockSpec(memory_space=pltpu.SMEM)
VMEM = pl.BlockSpec(memory_space=pltpu.VMEM)


def row_partials(chip_rows, weight, other_weight):
    chips = lax.axis_size("xl")
    rows, hidden = chip_rows[0].shape
    shard = weight.shape[0]
    ys = lax.axis_size("yh") * lax.axis_size("yl")
    inner = rows // ys

    def kernel(place, *refs):
        own, near, opposite, across, forwarded = refs[:5]
        weight_ref, other_ref, out_ref, stack_ref = refs[5:]
        chip, core = place[0], place[1]
        middle = jnp.logical_and(chip > 0, chip < chips - 1)
        stack_ref[chip] = own[...]
        stack_ref[chip ^ 1] = near[...]
        stack_ref[chip ^ 3] = opposite[...]

        @pl.when(middle)
        def _():
            stack_ref[chip ^ 2] = across[...]

        @pl.when(jnp.logical_not(middle))
        def _():
            stack_ref[chip ^ 2] = forwarded[...]

        blocks = stack_ref[...].reshape(chips * rows, hidden)
        for side, ref in ((core, weight_ref), (1 - core, other_ref)):
            part = lax.dot_general(
                blocks, ref[...], (((1,), (1,)), ((), ())), preferred_element_type=jnp.float32
            ).astype(jnp.bfloat16)
            columns = pl.ds(pl.multiple_of(side * shard, 128), shard)
            for chip_to in range(chips):
                for y in range(ys):
                    start = (chip_to * ys + y) * inner
                    out_ref[y, chip_to, :, columns] = part[start : start + inner]

    return pl.pallas_call(
        kernel,
        out_shape=(
            jax.ShapeDtypeStruct((ys, chips, inner, 2 * shard), jnp.bfloat16),
            jax.ShapeDtypeStruct((chips, rows, hidden), jnp.bfloat16),
        ),
        in_specs=[SMEM] + [VMEM] * (len(chip_rows) + 2),
        out_specs=(VMEM,) * 2,
        compiler_params=pltpu.CompilerParams(vmem_limit_bytes=VMEM_BYTES),
        cost_estimate=pl.CostEstimate(
            flops=8 * chips * rows * hidden * shard, bytes_accessed=6 << 20, transcendentals=0
        ),
        name="row_partials",
    )(
        place_of(lax.axis_index("xl"), lax.axis_index("core")),
        *chip_rows, weight, other_weight,
    )


def reduce_rows(partials):
    ys, chips, halves, experts, features = partials.shape

    def kernel(in_ref, out_ref):
        sums = []
        for chip in range(chips):
            total = jnp.zeros((experts, features), jnp.float32)
            for y in range(ys):
                for half in range(halves):
                    total += in_ref[y, chip, half].astype(jnp.float32)
            sums.append(total)
        out_ref[...] = jnp.stack(sums, axis=1).astype(jnp.bfloat16)

    return pl.pallas_call(
        kernel,
        out_shape=jax.ShapeDtypeStruct((experts, chips, features), jnp.bfloat16),
        in_specs=[VMEM],
        out_specs=VMEM,
        compiler_params=pltpu.CompilerParams(vmem_limit_bytes=VMEM_BYTES),
        cost_estimate=pl.CostEstimate(
            flops=ys * halves * chips * experts * features, bytes_accessed=1 << 20, transcendentals=0
        ),
        name="reduce_rows",
    )(partials)


def weight_gradient(pieces, chip_rows, other_rows):
    chips, rows, hidden = chip_rows.shape
    twins, shard = pieces[0].shape[0] // rows, pieces[0].shape[1]
    ys = len(pieces) * twins
    inner = rows // ys

    def kernel(place, *refs):
        piece_refs, (own_ref, other_ref, out_ref, layer) = refs[: len(pieces)], refs[len(pieces) :]
        core, pair = place[0], place[1]
        for away, ref in enumerate(piece_refs):
            for twin in range(twins):
                y = ((pair + away) & (len(pieces) - 1)) * twins + twin
                for chip in range(chips):
                    for c in range(2):
                        start = twin * rows + (chip * 2 + c) * inner
                        layer[core ^ c, chip, y] = ref[start : start + inner]
        contract = (((0,), (0,)), ((), ()))
        for n in range(0, hidden, 256):
            total = jnp.zeros((shard, 256), jnp.float32)
            for side, ref in enumerate((own_ref, other_ref)):
                total += lax.dot_general(
                    layer[side].reshape(chips * rows, shard),
                    ref[:, :, n : n + 256].reshape(chips * rows, 256),
                    contract,
                    preferred_element_type=jnp.float32,
                )
            out_ref[:, n : n + 256] = total.astype(jnp.bfloat16)

    return pl.pallas_call(
        kernel,
        out_shape=jax.ShapeDtypeStruct((shard, hidden), jnp.bfloat16),
        in_specs=[SMEM] + [VMEM] * (len(pieces) + 2),
        out_specs=VMEM,
        scratch_shapes=[pltpu.VMEM((2, chips, ys, inner, shard), jnp.bfloat16)],
        compiler_params=pltpu.CompilerParams(vmem_limit_bytes=VMEM_BYTES),
        cost_estimate=pl.CostEstimate(
            flops=4 * chips * rows * hidden * shard, bytes_accessed=6 << 20, transcendentals=0
        ),
        name="weight_gradient",
    )(place_of(lax.axis_index("core"), lax.axis_index("yh")), *pieces, chip_rows, other_rows)


def on_device(tokens, routes, up_weight, hidden_grad, gate_pre):
    chips, cores, experts = lax.axis_size("xl"), lax.axis_size("core"), lax.axis_size("ex")
    pairs, twins = lax.axis_size("yh"), lax.axis_size("yl")
    ys, halves = pairs * twins, lax.axis_size("h")
    owners = chips * cores
    token_count, width = tokens.shape
    _, shard, hidden = up_weight.shape
    rows = hidden_grad.shape[1]
    inner = halves * experts

    grad_up = derive(hidden_grad[0], gate_pre[0])
    grad_up = grad_up.reshape(experts, ys, halves, hidden).transpose(1, 2, 0, 3)
    grad_up = grad_up.reshape(rows, hidden)
    opposite = flip(grad_up, "xl", 3)
    across = lax.ppermute(grad_up, "xl", [(0, 2), (3, 1)])
    near = flip(grad_up, "xl", 1)
    forwarded = lax.ppermute(opposite, "xl", [(2, 3), (1, 0)])

    picks = jnp.any(
        routes[:, :, None] == jnp.arange(experts, dtype=jnp.int32)[None, None, :], axis=1
    ).astype(jnp.bfloat16)
    outgoing = jnp.einsum(
        "te,tqc->qec",
        picks,
        tokens.reshape(token_count, owners, shard),
        preferred_element_type=jnp.float32,
    ).astype(jnp.bfloat16)
    outgoing = jnp.broadcast_to(outgoing[:, None], (owners, halves, experts, shard))
    arrived = exchange(
        outgoing.reshape(owners * halves, experts, shard), ("xl", "core", "h")
    )
    weight = up_weight[0]
    other_weight = lax.ppermute(weight, "core", CORE_SWAP)
    arrived = jnp.broadcast_to(
        arrived.transpose(1, 0, 2)[:, None], (experts, twins, owners * halves, shard)
    )
    arrived = exchange(
        arrived.reshape(experts * twins, owners * halves, shard), ("ex", "yl")
    )
    arrived = arrived.reshape(experts, twins, owners, halves, shard).transpose(1, 2, 3, 0, 4)
    arrived = arrived.reshape(twins * rows, shard)

    partial, chip_rows = row_partials(
        (grad_up, near, opposite, across, forwarded), weight, other_weight
    )
    partial = exchange(
        partial.reshape(ys * chips * halves, experts, cores * shard), ("yh", "yl", "xl", "h")
    )
    row_grad = reduce_rows(partial.reshape(ys, chips, halves, experts, cores * shard))
    returned = exchange(row_grad, "ex")
    grad_tokens = jnp.einsum(
        "te,eqc->tqc", picks, returned, preferred_element_type=jnp.float32
    ).astype(jnp.bfloat16)

    pieces = [arrived]
    for _ in range(pairs // 2):
        pieces.append(shift(pieces[-1], "yh", -1))
    pieces.append(shift(arrived, "yh", 1))
    other_chip_rows = lax.ppermute(chip_rows, "core", CORE_SWAP)
    weight_grad = weight_gradient(pieces, chip_rows, other_chip_rows)
    return grad_tokens.reshape(token_count, width), weight_grad[None]


def solution(mesh):
    shape = (mesh.shape["dp"] // 2, 2, mesh.shape["expert"], mesh.shape["etensor"] // 4, 2, 2)
    fine = Mesh(mesh.devices.reshape(shape), ("xl", "core", "ex", "yh", "yl", "h"))
    tokens_spec = P(("xl", "core", "ex", "yh", "yl", "h"), None)
    expert_spec = P("ex", ("xl", "core"), ("yh", "yl", "h"))
    return jax.shard_map(
        on_device,
        mesh=fine,
        in_specs=(tokens_spec, tokens_spec, expert_spec, expert_spec, expert_spec),
        out_specs=(tokens_spec, expert_spec),
        check_vma=False,
    )
```

```python
import jax
import jax.numpy as jnp
from jax import lax
from jax.experimental import pallas as pl
from jax.experimental.pallas import tpu as pltpu
from jax.sharding import Mesh, PartitionSpec as P

CORE_SWAP = ((0, 1), (1, 0))
VMEM_BYTES = 40 * 1024 * 1024


def derive(grad_rows, gate_rows):
    gate_wide = gate_rows.astype(jnp.float32)
    sigma = jax.nn.sigmoid(gate_wide)
    return (grad_rows.astype(jnp.float32) * gate_wide * sigma).astype(jnp.bfloat16)


def exchange(blocks, axes):
    return lax.all_to_all(blocks, axes, split_axis=0, concat_axis=0, tiled=True)


def flip(value, axis, bits):
    return lax.ppermute(value, axis, [(i, i ^ bits) for i in range(lax.axis_size(axis))])


def shift(value, axis, by):
    size = lax.axis_size(axis)
    return lax.ppermute(value, axis, [(i, (i + by) % size) for i in range(size)])


def place_of(*indices):
    return jnp.stack(indices).astype(jnp.int32)


SMEM = pl.BlockSpec(memory_space=pltpu.SMEM)
VMEM = pl.BlockSpec(memory_space=pltpu.VMEM)


def row_partials(chip_rows, weight, other_weight):
    chips = lax.axis_size("xl")
    rows, hidden = chip_rows[0].shape
    shard = weight.shape[0]
    ys = lax.axis_size("yh") * lax.axis_size("yl")
    inner = rows // ys

    def kernel(place, *refs):
        own, near, opposite, across, forwarded = refs[:5]
        weight_ref, other_ref, out_ref, stack_ref = refs[5:]
        chip, core = place[0], place[1]
        middle = jnp.logical_and(chip > 0, chip < chips - 1)
        stack_ref[chip] = own[...]
        stack_ref[chip ^ 1] = near[...]
        stack_ref[chip ^ 3] = opposite[...]

        @pl.when(middle)
        def _():
            stack_ref[chip ^ 2] = across[...]

        @pl.when(jnp.logical_not(middle))
        def _():
            stack_ref[chip ^ 2] = forwarded[...]

        blocks = stack_ref[...].reshape(chips * rows, hidden)
        for side, ref in ((core, weight_ref), (1 - core, other_ref)):
            part = lax.dot_general(
                blocks, ref[...], (((1,), (1,)), ((), ())), preferred_element_type=jnp.float32
            ).astype(jnp.bfloat16)
            columns = pl.ds(pl.multiple_of(side * shard, 128), shard)
            for chip_to in range(chips):
                for y in range(ys):
                    start = (chip_to * ys + y) * inner
                    out_ref[y, chip_to, :, columns] = part[start : start + inner]

    return pl.pallas_call(
        kernel,
        out_shape=(
            jax.ShapeDtypeStruct((ys, chips, inner, 2 * shard), jnp.bfloat16),
            jax.ShapeDtypeStruct((chips, rows, hidden), jnp.bfloat16),
        ),
        in_specs=[SMEM] + [VMEM] * (len(chip_rows) + 2),
        out_specs=(VMEM,) * 2,
        compiler_params=pltpu.CompilerParams(vmem_limit_bytes=VMEM_BYTES),
        cost_estimate=pl.CostEstimate(
            flops=8 * chips * rows * hidden * shard, bytes_accessed=6 << 20, transcendentals=0
        ),
        name="row_partials",
    )(
        place_of(lax.axis_index("xl"), lax.axis_index("core")),
        *chip_rows, weight, other_weight,
    )


def reduce_rows(partials):
    ys, chips, halves, experts, features = partials.shape

    def kernel(in_ref, out_ref):
        sums = []
        for chip in range(chips):
            total = jnp.zeros((experts, features), jnp.float32)
            for y in range(ys):
                for half in range(halves):
                    total += in_ref[y, chip, half].astype(jnp.float32)
            sums.append(total)
        out_ref[...] = jnp.stack(sums, axis=1).astype(jnp.bfloat16)

    return pl.pallas_call(
        kernel,
        out_shape=jax.ShapeDtypeStruct((experts, chips, features), jnp.bfloat16),
        in_specs=[VMEM],
        out_specs=VMEM,
        compiler_params=pltpu.CompilerParams(vmem_limit_bytes=VMEM_BYTES),
        cost_estimate=pl.CostEstimate(
            flops=ys * halves * chips * experts * features, bytes_accessed=1 << 20, transcendentals=0
        ),
        name="reduce_rows",
    )(partials)


def weight_gradient(pieces, aways, chip_rows, other_rows):
    chips, rows, hidden = chip_rows.shape
    twins, shard = pieces[0].shape[0] // rows, pieces[0].shape[1]
    ys = len(pieces) * twins
    inner = rows // ys

    def kernel(place, *refs):
        piece_refs, (own_ref, other_ref, out_ref, layer) = refs[: len(pieces)], refs[len(pieces) :]
        core, pair = place[0], place[1]
        for away, ref in zip(aways, piece_refs):
            for twin in range(twins):
                y = ((pair + away) & (len(pieces) - 1)) * twins + twin
                for chip in range(chips):
                    for c in range(2):
                        start = twin * rows + (chip * 2 + c) * inner
                        layer[core ^ c, chip, y] = ref[start : start + inner]
        contract = (((0,), (0,)), ((), ()))
        for n in range(0, hidden, 256):
            total = jnp.zeros((shard, 256), jnp.float32)
            for side, ref in enumerate((own_ref, other_ref)):
                total += lax.dot_general(
                    layer[side].reshape(chips * rows, shard),
                    ref[:, :, n : n + 256].reshape(chips * rows, 256),
                    contract,
                    preferred_element_type=jnp.float32,
                )
            out_ref[:, n : n + 256] = total.astype(jnp.bfloat16)

    return pl.pallas_call(
        kernel,
        out_shape=jax.ShapeDtypeStruct((shard, hidden), jnp.bfloat16),
        in_specs=[SMEM] + [VMEM] * (len(pieces) + 2),
        out_specs=VMEM,
        scratch_shapes=[pltpu.VMEM((2, chips, ys, inner, shard), jnp.bfloat16)],
        compiler_params=pltpu.CompilerParams(vmem_limit_bytes=VMEM_BYTES),
        cost_estimate=pl.CostEstimate(
            flops=4 * chips * rows * hidden * shard, bytes_accessed=6 << 20, transcendentals=0
        ),
        name="weight_gradient",
    )(place_of(lax.axis_index("core"), lax.axis_index("yh")), *pieces, chip_rows, other_rows)


def on_device(tokens, routes, up_weight, hidden_grad, gate_pre):
    chips, cores, experts = lax.axis_size("xl"), lax.axis_size("core"), lax.axis_size("ex")
    pairs, twins = lax.axis_size("yh"), lax.axis_size("yl")
    ys, halves = pairs * twins, lax.axis_size("h")
    owners = chips * cores
    token_count, width = tokens.shape
    _, shard, hidden = up_weight.shape
    rows = hidden_grad.shape[1]
    inner = halves * experts

    grad_up = derive(hidden_grad[0], gate_pre[0])
    grad_up = grad_up.reshape(experts, ys, halves, hidden).transpose(1, 2, 0, 3)
    grad_up = grad_up.reshape(rows, hidden)
    opposite = flip(grad_up, "xl", 3)
    across = lax.ppermute(grad_up, "xl", [(0, 2), (3, 1)])
    near = flip(grad_up, "xl", 1)
    forwarded = lax.ppermute(opposite, "xl", [(2, 3), (1, 0)])

    picks = jnp.any(
        routes[:, :, None] == jnp.arange(experts, dtype=jnp.int32)[None, None, :], axis=1
    ).astype(jnp.bfloat16)
    outgoing = jnp.einsum(
        "te,tqc->qec",
        picks,
        tokens.reshape(token_count, owners, shard),
        preferred_element_type=jnp.float32,
    ).astype(jnp.bfloat16)
    outgoing = jnp.broadcast_to(outgoing[:, None], (owners, halves, experts, shard))
    arrived = exchange(
        outgoing.reshape(owners * halves, experts, shard), ("xl", "core", "h")
    )
    weight = up_weight[0]
    other_weight = lax.ppermute(weight, "core", CORE_SWAP)
    arrived = jnp.broadcast_to(
        arrived.transpose(1, 0, 2)[:, None], (experts, twins, owners * halves, shard)
    )
    arrived = exchange(
        arrived.reshape(experts * twins, owners * halves, shard), ("ex", "yl")
    )
    arrived = arrived.reshape(experts, twins, owners, halves, shard).transpose(1, 2, 3, 0, 4)
    arrived = arrived.reshape(twins * rows, shard)

    partial, chip_rows = row_partials(
        (grad_up, near, opposite, across, forwarded), weight, other_weight
    )
    partial = exchange(
        partial.reshape(ys * chips * halves, experts, cores * shard), ("yh", "yl", "xl", "h")
    )
    row_grad = reduce_rows(partial.reshape(ys, chips, halves, experts, cores * shard))
    returned = exchange(row_grad, "ex")
    grad_tokens = jnp.einsum(
        "te,eqc->tqc", picks, returned, preferred_element_type=jnp.float32
    ).astype(jnp.bfloat16)

    aways = (0, pairs // 2, pairs - 1, 1)
    pieces = [arrived] + [shift(arrived, "yh", -away) for away in aways[1:]]
    other_chip_rows = lax.ppermute(chip_rows, "core", CORE_SWAP)
    weight_grad = weight_gradient(pieces, aways, chip_rows, other_chip_rows)
    return grad_tokens.reshape(token_count, width), weight_grad[None]


def solution(mesh):
    shape = (mesh.shape["dp"] // 2, 2, mesh.shape["expert"], mesh.shape["etensor"] // 4, 2, 2)
    fine = Mesh(mesh.devices.reshape(shape), ("xl", "core", "ex", "yh", "yl", "h"))
    tokens_spec = P(("xl", "core", "ex", "yh", "yl", "h"), None)
    expert_spec = P("ex", ("xl", "core"), ("yh", "yl", "h"))
    return jax.shard_map(
        on_device,
        mesh=fine,
        in_specs=(tokens_spec, tokens_spec, expert_spec, expert_spec, expert_spec),
        out_specs=(tokens_spec, expert_spec),
        check_vma=False,
    )
```

```python
import jax
import jax.numpy as jnp
from jax import lax
from jax.experimental import pallas as pl
from jax.experimental.pallas import tpu as pltpu
from jax.sharding import Mesh, PartitionSpec as P

CORE_SWAP = ((0, 1), (1, 0))
VMEM_BYTES = 40 * 1024 * 1024


def derive(grad_rows, gate_rows):
    gate_wide = gate_rows.astype(jnp.float32)
    sigma = jax.nn.sigmoid(gate_wide)
    return (grad_rows.astype(jnp.float32) * gate_wide * sigma).astype(jnp.bfloat16)


def exchange(blocks, axes):
    return lax.all_to_all(blocks, axes, split_axis=0, concat_axis=0, tiled=True)


def flip(value, axis, bits):
    return lax.ppermute(value, axis, [(i, i ^ bits) for i in range(lax.axis_size(axis))])


def shift(value, axis, by):
    size = lax.axis_size(axis)
    return lax.ppermute(value, axis, [(i, (i + by) % size) for i in range(size)])


def place_of(*indices):
    return jnp.stack(indices).astype(jnp.int32)


SMEM = pl.BlockSpec(memory_space=pltpu.SMEM)
VMEM = pl.BlockSpec(memory_space=pltpu.VMEM)


def row_partials(chip_rows, weight, other_weight):
    chips = lax.axis_size("xl")
    rows, hidden = chip_rows[0].shape
    shard = weight.shape[0]
    ys = lax.axis_size("yh") * lax.axis_size("yl")
    inner = rows // ys

    def kernel(place, *refs):
        own, near, opposite, across, forwarded = refs[:5]
        weight_ref, other_ref, out_ref, stack_ref = refs[5:]
        chip, core = place[0], place[1]
        middle = jnp.logical_and(chip > 0, chip < chips - 1)
        stack_ref[chip] = own[...]
        stack_ref[chip ^ 1] = near[...]
        stack_ref[chip ^ 3] = opposite[...]

        @pl.when(middle)
        def _():
            stack_ref[chip ^ 2] = across[...]

        @pl.when(jnp.logical_not(middle))
        def _():
            stack_ref[chip ^ 2] = forwarded[...]

        blocks = stack_ref[...].reshape(chips * rows, hidden)
        for side, ref in ((core, weight_ref), (1 - core, other_ref)):
            part = lax.dot_general(
                blocks, ref[...], (((1,), (1,)), ((), ())), preferred_element_type=jnp.float32
            ).astype(jnp.bfloat16)
            columns = pl.ds(pl.multiple_of(side * shard, 128), shard)
            for chip_to in range(chips):
                for y in range(ys):
                    start = (chip_to * ys + y) * inner
                    out_ref[y, chip_to, :, columns] = part[start : start + inner]

    return pl.pallas_call(
        kernel,
        out_shape=(
            jax.ShapeDtypeStruct((ys, chips, inner, 2 * shard), jnp.bfloat16),
            jax.ShapeDtypeStruct((chips, rows, hidden), jnp.bfloat16),
        ),
        in_specs=[SMEM] + [VMEM] * (len(chip_rows) + 2),
        out_specs=(VMEM,) * 2,
        compiler_params=pltpu.CompilerParams(vmem_limit_bytes=VMEM_BYTES),
        cost_estimate=pl.CostEstimate(
            flops=8 * chips * rows * hidden * shard, bytes_accessed=6 << 20, transcendentals=0
        ),
        name="row_partials",
    )(
        place_of(lax.axis_index("xl"), lax.axis_index("core")),
        *chip_rows, weight, other_weight,
    )


def reduce_rows(partials):
    ys, chips, halves, experts, features = partials.shape

    def kernel(in_ref, out_ref):
        sums = []
        for chip in range(chips):
            total = jnp.zeros((experts, features), jnp.float32)
            for y in range(ys):
                for half in range(halves):
                    total += in_ref[y, chip, half].astype(jnp.float32)
            sums.append(total)
        out_ref[...] = jnp.stack(sums, axis=1).astype(jnp.bfloat16)

    return pl.pallas_call(
        kernel,
        out_shape=jax.ShapeDtypeStruct((experts, chips, features), jnp.bfloat16),
        in_specs=[VMEM],
        out_specs=VMEM,
        compiler_params=pltpu.CompilerParams(vmem_limit_bytes=VMEM_BYTES),
        cost_estimate=pl.CostEstimate(
            flops=ys * halves * chips * experts * features, bytes_accessed=1 << 20, transcendentals=0
        ),
        name="reduce_rows",
    )(partials)


def weight_gradient(pieces, aways, chip_rows, other_rows):
    chips, rows, hidden = chip_rows.shape
    twins, shard = pieces[0].shape[0] // rows, pieces[0].shape[1]
    ys = len(pieces) * twins
    inner = rows // ys

    def kernel(place, *refs):
        piece_refs, (own_ref, other_ref, out_ref, layer) = refs[: len(pieces)], refs[len(pieces) :]
        core, pair = place[0], place[1]
        for away, ref in zip(aways, piece_refs):
            for twin in range(twins):
                y = ((pair + away) & (len(pieces) - 1)) * twins + twin
                for chip in range(chips):
                    for c in range(2):
                        start = twin * rows + (chip * 2 + c) * inner
                        layer[core ^ c, chip, y] = ref[start : start + inner]
        contract = (((0,), (0,)), ((), ()))
        for n in range(0, hidden, 256):
            total = jnp.zeros((shard, 256), jnp.float32)
            for side, ref in enumerate((own_ref, other_ref)):
                total += lax.dot_general(
                    layer[side].reshape(chips * rows, shard),
                    ref[:, :, n : n + 256].reshape(chips * rows, 256),
                    contract,
                    preferred_element_type=jnp.float32,
                )
            out_ref[:, n : n + 256] = total.astype(jnp.bfloat16)

    return pl.pallas_call(
        kernel,
        out_shape=jax.ShapeDtypeStruct((shard, hidden), jnp.bfloat16),
        in_specs=[SMEM] + [VMEM] * (len(pieces) + 2),
        out_specs=VMEM,
        scratch_shapes=[pltpu.VMEM((2, chips, ys, inner, shard), jnp.bfloat16)],
        compiler_params=pltpu.CompilerParams(vmem_limit_bytes=VMEM_BYTES),
        cost_estimate=pl.CostEstimate(
            flops=4 * chips * rows * hidden * shard, bytes_accessed=6 << 20, transcendentals=0
        ),
        name="weight_gradient",
    )(place_of(lax.axis_index("core"), lax.axis_index("yh")), *pieces, chip_rows, other_rows)


def on_device(tokens, routes, up_weight, hidden_grad, gate_pre):
    chips, cores, experts = lax.axis_size("xl"), lax.axis_size("core"), lax.axis_size("ex")
    pairs, twins = lax.axis_size("yh"), lax.axis_size("yl")
    ys, halves = pairs * twins, lax.axis_size("h")
    owners = chips * cores
    token_count, width = tokens.shape
    _, shard, hidden = up_weight.shape
    rows = hidden_grad.shape[1]
    inner = halves * experts

    grad_up = derive(hidden_grad[0], gate_pre[0])
    grad_up = grad_up.reshape(experts, ys, halves, hidden).transpose(1, 2, 0, 3)
    grad_up = grad_up.reshape(rows, hidden)
    opposite = flip(grad_up, "xl", 3)
    across = lax.ppermute(grad_up, "xl", [(0, 2), (3, 1)])
    near = flip(grad_up, "xl", 1)
    forwarded = lax.ppermute(opposite, "xl", [(2, 3), (1, 0)])

    picks = jnp.any(
        routes[:, :, None] == jnp.arange(experts, dtype=jnp.int32)[None, None, :], axis=1
    ).astype(jnp.bfloat16)
    outgoing = jnp.einsum(
        "te,tqc->qec",
        picks,
        tokens.reshape(token_count, owners, shard),
        preferred_element_type=jnp.float32,
    ).astype(jnp.bfloat16)
    outgoing = jnp.broadcast_to(outgoing[:, None], (owners, halves, experts, shard))
    arrived = exchange(
        outgoing.reshape(owners * halves, experts, shard), ("xl", "core", "h")
    )
    weight = up_weight[0]
    other_weight = lax.ppermute(weight, "core", CORE_SWAP)
    arrived = jnp.broadcast_to(
        arrived.transpose(1, 0, 2)[:, None], (experts, twins, owners * halves, shard)
    )
    arrived = exchange(
        arrived.reshape(experts * twins, owners * halves, shard), ("ex", "yl")
    )
    arrived = arrived.reshape(experts, twins, owners, halves, shard).transpose(1, 2, 3, 0, 4)
    arrived = arrived.reshape(twins * rows, shard)

    partial, chip_rows = row_partials(
        (grad_up, near, opposite, across, forwarded), weight, other_weight
    )
    partial = exchange(
        partial.reshape(ys * chips * halves, experts, cores * shard), ("yh", "yl", "xl", "h")
    )
    row_grad = reduce_rows(partial.reshape(ys, chips, halves, experts, cores * shard))
    returned = exchange(row_grad, "ex")
    grad_tokens = jnp.einsum(
        "te,eqc->tqc", picks, returned, preferred_element_type=jnp.float32
    ).astype(jnp.bfloat16)

    aways = (0, pairs // 2, pairs - 1, 1)
    pieces = [arrived] + [shift(arrived, "yh", -away) for away in aways[1:]]
    other_chip_rows = lax.ppermute(chip_rows, "core", CORE_SWAP)
    grad_tokens, other_chip_rows = lax.optimization_barrier((grad_tokens, other_chip_rows))
    weight_grad = weight_gradient(pieces, aways, chip_rows, other_chip_rows)
    return grad_tokens.reshape(token_count, width), weight_grad[None]


def solution(mesh):
    shape = (mesh.shape["dp"] // 2, 2, mesh.shape["expert"], mesh.shape["etensor"] // 4, 2, 2)
    fine = Mesh(mesh.devices.reshape(shape), ("xl", "core", "ex", "yh", "yl", "h"))
    tokens_spec = P(("xl", "core", "ex", "yh", "yl", "h"), None)
    expert_spec = P("ex", ("xl", "core"), ("yh", "yl", "h"))
    return jax.shard_map(
        on_device,
        mesh=fine,
        in_specs=(tokens_spec, tokens_spec, expert_spec, expert_spec, expert_spec),
        out_specs=(tokens_spec, expert_spec),
        check_vma=False,
    )
```
